32 devices in a mesh: replica: 4 (over y, x), shard: 8 (over z, core).
Axes of the slice: x: 2, y: 2, z: 4, core: 2. Of those that a mesh axis runs over, the one named last changes fastest.
Arguments:
- tokens: bfloat16 [24576, 960], P(('replica', 'shard')), may hold values from -6 to 6
- cotangent: bfloat16 [24576, 960], P(('replica', 'shard')), may hold values from -6 to 6
- seq_lengths: int32 [32, 4], P(('replica', 'shard')), may hold values from 0 to 512, as said below
- w_query: bfloat16 [960, 960], P('shard'), may hold values from -0.1875 to 0.1875
- key_weight: bfloat16 [960, 320], P('shard'), may hold values from -0.1875 to 0.1875
- value_weight: bfloat16 [960, 320], P('shard'), may hold values from -0.1875 to 0.1875
- w_out: bfloat16 [960, 960], P('shard'), may hold values from -0.75 to 0.75
- w_gate: bfloat16 [960, 2560], P('shard'), may hold values from -0.1875 to 0.1875
- w_up: bfloat16 [960, 2560], P('shard'), may hold values from -0.1875 to 0.1875
- w_down: bfloat16 [2560, 960], P('shard'), may hold values from -0.125 to 0.125
- gain_attn: bfloat16 [960], P('shard'), may hold values from 0.5 to 1.5
- gain_ffn: bfloat16 [960], P('shard'), may hold values from 0.5 to 1.5
Outputs:
- output: bfloat16 [24576, 960], P(('replica', 'shard'))
- grad_tokens: bfloat16 [24576, 960], P(('replica', 'shard'))
- grad_query: float32 [960, 960], P('shard')
- grad_key: float32 [960, 320], P('shard')
- grad_value: float32 [960, 320], P('shard')
- grad_out: float32 [960, 960], P('shard')
- grad_gate: float32 [960, 2560], P('shard')
- grad_up: float32 [960, 2560], P('shard')
- grad_down: float32 [2560, 960], P('shard')
- grad_gain_attn: float32 [960], P('shard')
- grad_gain_ffn: float32 [960], P('shard')
The draws below stay inside these ranges and needn't reach their ends.
Inputs may be any that keep to these rules, and one draw needn't show every extreme that they name: `seq_lengths`: the lengths of one buffer sum to at most 768; unused slots hold 0; some buffer holds one sequence of exactly 512.
All inputs are finite; a program needn't handle non-finite values.
Results may differ from the reference program's by a relative error of at most 0.014.
Values may be sent and summed in bfloat16 or wider, within the bound.
A program may use at most 256 MiB of HBM per device.

```python
import jax
import jax.numpy as jnp
from jax import lax

MODEL_WIDTH = 960
QUERY_HEADS = 15
KEY_VALUE_HEADS = 5
HEAD_SIZE = 64
FF = 2560
ROWS_DEV = 768
SEQ_DEV = 4
MAXLEN = 512
BUFFERS = 32
TOKENS = 24576


def draw_seq_lengths(key, part):
    key = jax.random.fold_in(key, 11)
    key_live, key_proposed, key_pick = jax.random.split(key, 3)
    filled = jax.random.randint(key_live, (BUFFERS,), ROWS_DEV // 3, ROWS_DEV + 1)
    proposed = jax.random.randint(key_proposed, (BUFFERS, SEQ_DEV), 1, MAXLEN + 1)
    before = jnp.cumsum(proposed, axis=1) - proposed
    space_left = jnp.maximum(filled[:, None] - before, 0)
    clipped = jnp.minimum(proposed, space_left)
    chosen = jax.random.randint(key_pick, (), 0, BUFFERS)
    single = jnp.where(jnp.arange(SEQ_DEV) == 0, MAXLEN, 0)
    buffer_ids = jnp.arange(BUFFERS)
    return jnp.where((buffer_ids == chosen)[:, None], single[None, :], clipped).astype(jnp.int32)


def level_of(own_key, dims, pieces, smallest, top_value):
    loudness, own = 1.0, jax.random.fold_in(own_key, 6)
    for axis_at, shards_of in pieces:
        steps = jnp.exp(jax.random.uniform(jax.random.fold_in(own, axis_at), (shards_of,), jnp.float32, smallest / len(pieces), top_value / len(pieces)))
        loudness = loudness * jnp.repeat(steps, dims[axis_at] // shards_of).reshape([-1 if axis == axis_at else 1 for axis in range(len(dims))])
    return loudness


def noise(rng, dims, scale, bound, shards=(), kind=jnp.bfloat16):
    loudness = level_of(rng, dims, shards, -0.22, 0.18) if shards else 1.0
    result = jax.random.normal(rng, dims, jnp.float32) * scale * loudness
    return jnp.minimum(jnp.maximum(result, -bound), bound).astype(kind)


def setup_inputs(seed: int = 0) -> dict:
    streams_of = jax.random.split(jax.random.key(seed), 13)
    tokens = noise(streams_of[0], (TOKENS, MODEL_WIDTH), 1.0, 6.0, ((0, 32),))
    cotangent = noise(streams_of[1], (TOKENS, MODEL_WIDTH), 1.0, 6.0, ((0, 32),))
    seq_lengths = draw_seq_lengths(jax.random.fold_in(streams_of[12], 71), 0)
    w_query = noise(streams_of[3], (MODEL_WIDTH, QUERY_HEADS * HEAD_SIZE), MODEL_WIDTH ** -0.5, 0.1875, ((0, 8),))
    key_weight = noise(streams_of[4], (MODEL_WIDTH, KEY_VALUE_HEADS * HEAD_SIZE), MODEL_WIDTH ** -0.5, 0.1875, ((0, 8),))
    value_weight = noise(streams_of[5], (MODEL_WIDTH, KEY_VALUE_HEADS * HEAD_SIZE), MODEL_WIDTH ** -0.5, 0.1875, ((0, 8),))
    w_out = noise(streams_of[6], (QUERY_HEADS * HEAD_SIZE, MODEL_WIDTH), (QUERY_HEADS * HEAD_SIZE // 16) ** -0.5, 0.75, ((0, 8),))
    w_gate = noise(streams_of[7], (MODEL_WIDTH, FF), MODEL_WIDTH ** -0.5, 0.1875, ((0, 8),))
    w_up = noise(streams_of[8], (MODEL_WIDTH, FF), MODEL_WIDTH ** -0.5, 0.1875, ((0, 8),))
    w_down = noise(streams_of[9], (FF, MODEL_WIDTH), FF ** -0.5, 0.125, ((0, 8),))
    gain_attn = jnp.clip(1.0 + 0.1 * jax.random.normal(streams_of[10], (MODEL_WIDTH,), jnp.float32), 0.5, 1.5).astype(jnp.bfloat16)
    gain_ffn = jnp.clip(1.0 + 0.1 * jax.random.normal(streams_of[11], (MODEL_WIDTH,), jnp.float32), 0.5, 1.5).astype(jnp.bfloat16)
    return {"tokens": tokens, "cotangent": cotangent, "seq_lengths": seq_lengths, "w_query": w_query, "key_weight": key_weight, "value_weight": value_weight, "w_out": w_out, "w_gate": w_gate, "w_up": w_up, "w_down": w_down, "gain_attn": gain_attn, "gain_ffn": gain_ffn}


@jax.custom_vjp
def reduced_precision(v):
    return lax.optimization_barrier(v.astype(jnp.bfloat16)).astype(jnp.float32)

@jax.custom_vjp
def reduced_backward(v):
    return v

def low_keep(v):
    return (reduced_precision(v), None)

def low_pass(kept, grad):
    return (grad,)

def back_keep(v):
    return (v, None)

def back_low(kept, grad):
    return (reduced_precision(grad),)
reduced_precision.defvjp(low_keep, low_pass)
reduced_backward.defvjp(back_keep, back_low)

def layout(lengths_row, token_rows):
    seq_ends = jnp.cumsum(lengths_row)
    positions = jnp.arange(token_rows, dtype=jnp.int32)
    passed = positions[:, None] >= seq_ends[None, :]
    segment = lax.optimization_barrier(jnp.sum(passed.astype(jnp.int32), axis=1))
    seq_start = lax.optimization_barrier(jnp.sum(jnp.where(passed, lengths_row[None, :], 0), axis=1))
    offset = (positions - seq_start).astype(jnp.float32)
    living = positions < seq_ends[-1]
    allowed = (segment[:, None] == segment[None, :]) & (positions[None, :] <= positions[:, None]) & living[:, None]
    allowed = allowed | (positions[:, None] == positions[None, :])
    return (offset, living.astype(jnp.float32), allowed)

def rotation(offset, half_dim):
    frequency = 10000.0 ** (-jnp.arange(half_dim, dtype=jnp.float32) / half_dim)
    angles = offset[:, None] * frequency[None, :]
    return (jnp.cos(angles)[:, None, :], jnp.sin(angles)[:, None, :])

def apply_rotary(values, cosine_table, sine_table):
    half_dim = values.shape[-1] // 2
    leading = values[..., :half_dim]
    trailing = values[..., half_dim:]
    return jnp.concatenate([leading * cosine_table - trailing * sine_table, trailing * cosine_table + leading * sine_table], axis=-1)

def rms_scale(values):
    return lax.rsqrt(lax.optimization_barrier(jnp.mean(values * values, axis=-1, keepdims=True)) + 1e-05)

def matrix_multiply(left, right):
    return jnp.dot(left, right, precision=lax.Precision.HIGHEST)

def block(tokens_f, lengths_row, params):
    w_query, key_weight, value_weight, w_out, w_gate, w_up, w_down, gain_attn, gain_ffn = params
    token_rows = tokens_f.shape[0]
    offset, living, allowed = layout(lengths_row, token_rows)
    cosine_table, sine_table = rotation(offset, HEAD_SIZE // 2)
    masked = tokens_f * living[:, None]
    normalized_input = reduced_precision(masked * rms_scale(masked) * gain_attn)
    query_rows = matrix_multiply(normalized_input, w_query).reshape(token_rows, QUERY_HEADS, HEAD_SIZE)
    unrotated_keys = matrix_multiply(normalized_input, key_weight).reshape(token_rows, KEY_VALUE_HEADS, HEAD_SIZE)
    projected_values = matrix_multiply(normalized_input, value_weight).reshape(token_rows, KEY_VALUE_HEADS, HEAD_SIZE)
    rotated_query = reduced_precision(apply_rotary(reduced_backward(query_rows), cosine_table, sine_table)).reshape(token_rows, KEY_VALUE_HEADS, QUERY_HEADS // KEY_VALUE_HEADS, HEAD_SIZE)
    k_rot = reduced_precision(apply_rotary(reduced_backward(unrotated_keys), cosine_table, sine_table))
    v_low = reduced_precision(reduced_backward(projected_values))
    scores = reduced_backward(jnp.einsum('ikgd,jkd->kgij', rotated_query, k_rot, precision=lax.Precision.HIGHEST) * 0.125)
    shifted = jnp.where(allowed, scores, -1e+30)
    peak = lax.optimization_barrier(jnp.max(shifted, axis=-1, keepdims=True))
    raised = jnp.exp(shifted - peak)
    probs = raised / lax.optimization_barrier(jnp.sum(raised, axis=-1, keepdims=True))
    attended = jnp.einsum('kgij,jkd->ikgd', reduced_precision(probs), v_low, precision=lax.Precision.HIGHEST).reshape(token_rows, QUERY_HEADS * HEAD_SIZE)
    attn_out = reduced_backward(matrix_multiply(reduced_precision(reduced_backward(attended)), w_out))
    middle = masked + attn_out
    normed_two = reduced_precision(middle * rms_scale(middle) * gain_ffn)
    gate = reduced_backward(matrix_multiply(normed_two, w_gate))
    up_proj = reduced_backward(matrix_multiply(normed_two, w_up))
    hidden = reduced_precision(gate * jax.nn.sigmoid(gate) * up_proj)
    ffn_out = reduced_backward(matrix_multiply(hidden, w_down))
    return living[:, None] * (middle + ffn_out)

def reference(tokens, cotangent, seq_lengths, w_query, key_weight, value_weight, w_out, w_gate, w_up, w_down, gain_attn, gain_ffn):
    params = (w_query.astype(jnp.float32), key_weight.astype(jnp.float32), value_weight.astype(jnp.float32), w_out.astype(jnp.float32), w_gate.astype(jnp.float32), w_up.astype(jnp.float32), w_down.astype(jnp.float32), gain_attn.astype(jnp.float32), gain_ffn.astype(jnp.float32))
    stacked = tokens.astype(jnp.float32).reshape(BUFFERS, ROWS_DEV, MODEL_WIDTH)
    cot_stacked = cotangent.astype(jnp.float32).reshape(BUFFERS, ROWS_DEV, MODEL_WIDTH)

    def forward(stacked_in, weights_in):

        def one_buffer(item):
            return block(item[0], item[1], weights_in)
        return lax.map(jax.checkpoint(one_buffer), (stacked_in, seq_lengths))
    outputs, pullback = jax.vjp(forward, stacked, params)
    grad_stacked, grad_params = pullback(cot_stacked)
    return (outputs.reshape(TOKENS, MODEL_WIDTH).astype(jnp.bfloat16), grad_stacked.reshape(TOKENS, MODEL_WIDTH).astype(jnp.bfloat16), grad_params[0], grad_params[1], grad_params[2], grad_params[3], grad_params[4], grad_params[5], grad_params[6], grad_params[7], grad_params[8])
```

```python
import jax
import jax.numpy as jnp
from jax import lax
from jax.sharding import PartitionSpec as P

QUERY_HEADS = 15
KEY_VALUE_HEADS = 5
HEAD_SIZE = 64


AXES = ("replica", "shard")


def cells():
    replicas = lax.axis_size("replica")
    shards = lax.axis_size("shard")
    return replicas, shards, lax.axis_index("replica"), lax.axis_index("shard")


def swap(value, kind, bit):
    replicas, shards, _, _ = cells()
    pairs = []
    for r in range(replicas):
        for s in range(shards):
            to = (r ^ bit) * shards + s if kind == "r" else r * shards + (s ^ bit)
            pairs.append((r * shards + s, to))
    return lax.ppermute(value, AXES, pairs)


def my_bit(kind, bit):
    _, _, r, s = cells()
    return ((r if kind == "r" else s) // bit) % 2


def bits_of(size):
    found = []
    bit = 1
    while bit < size:
        found.append(bit)
        bit *= 2
    return found


def low(value):
    return lax.reduce_precision(value.astype(jnp.float32), 8, 7).astype(jnp.bfloat16)


class Spread:
    def __init__(self, parts):
        self.parts = parts

    def axis(self, part):
        return self.parts.index(part)


def grow(value, spread, part):
    axis = spread.axis(part)
    other = swap(value, *part)
    upper = my_bit(*part) == 1
    first = jnp.where(upper, other, value)
    second = jnp.where(upper, value, other)
    return jnp.concatenate([first, second], axis=axis)


def halve(value, spread, part):
    axis = spread.axis(part)
    upper = my_bit(*part) == 1
    lower_half = lax.slice_in_dim(value, 0, 1, axis=axis)
    upper_half = lax.slice_in_dim(value, 1, 2, axis=axis)
    keep = jnp.where(upper, upper_half, lower_half)
    send = jnp.where(upper, lower_half, upper_half)
    other = swap(low(send), *part)
    return keep.astype(jnp.float32) + other.astype(jnp.float32)


def both(value, part):
    mine = low(value)
    return mine.astype(jnp.float32) + swap(mine, *part).astype(jnp.float32)


def shard_parts():
    _, shards, _, _ = cells()
    return [("s", bit) for bit in reversed(bits_of(shards))]


def replica_parts():
    replicas, _, _, _ = cells()
    return [("r", bit) for bit in reversed(bits_of(replicas))]


def gather_rows(block):
    parts = shard_parts()
    spread = Spread(parts)
    value = block.reshape((1,) * len(parts) + block.shape)
    for part in parts:
        value = grow(value, spread, part)
    return value.reshape((-1, block.shape[1]))


def gather_split(block, split_rows, order):
    shard_bits = shard_parts()
    replica_bits = replica_parts()
    replicas, shards, r, _ = cells()
    rows, columns = block.shape
    parts = shard_bits + replica_bits
    spread = Spread(parts)
    if split_rows:
        piece = lax.dynamic_slice_in_dim(block, r * (rows // replicas), rows // replicas, axis=0)
    else:
        piece = lax.dynamic_slice_in_dim(block, r * (columns // replicas), columns // replicas, axis=1)
    value = piece.reshape((1,) * len(parts) + piece.shape)
    for part in order(shard_bits, replica_bits):
        value = grow(value, spread, part)
    value = value.reshape((shards, replicas) + piece.shape)
    if not split_rows:
        value = jnp.concatenate([value[:, i] for i in range(replicas)], axis=-1)
    return value.reshape(shards * rows, columns)


def reduce_rows(grad):
    parts = shard_parts()
    spread = Spread(parts)
    _, shards, _, _ = cells()
    rows, columns = grad.shape
    value = grad.reshape((2,) * len(parts) + (rows // shards, columns))
    for part in reversed(parts):
        value = halve(value, spread, part)
    value = value.reshape(rows // shards, columns)
    for part in replica_parts():
        value = both(value, part)
    return value


def reduce_split(grad, split_rows, order):
    shard_bits = shard_parts()
    replica_bits = replica_parts()
    replicas, shards, _, _ = cells()
    rows, columns = grad.shape
    own = rows // shards
    parts = shard_bits + replica_bits
    spread = Spread(parts)
    if split_rows:
        value = grad.reshape((2,) * len(parts) + (own // replicas, columns))
    else:
        width = columns // replicas
        value = jnp.stack(
            [grad[:, i * width : (i + 1) * width].reshape(shards, own, width) for i in range(replicas)],
            axis=1,
        ).reshape((2,) * len(parts) + (own, width))
    done = []
    for part in order(shard_bits, replica_bits):
        value = halve(value, spread, part)
        if part[0] == "r":
            done.append(part)
    value = low(value)
    for part in reversed(done):
        value = grow(value, spread, part)
    value = value.reshape((replicas,) + value.shape[-2:])
    if not split_rows:
        value = jnp.concatenate([value[i] for i in range(replicas)], axis=-1)
    return value.reshape(own, columns).astype(jnp.float32)


def gather_zxy(shard_bits, replica_bits):
    return shard_bits[:-1] + replica_bits + shard_bits[-1:]


def gather_zyx(shard_bits, replica_bits):
    return shard_bits[:-1] + replica_bits[::-1] + shard_bits[-1:]


def gather_xyz(shard_bits, replica_bits):
    return shard_bits[:1] + replica_bits + shard_bits[1:]


def reduce_xyz(shard_bits, replica_bits):
    return shard_bits[-1:] + replica_bits + shard_bits[:-1][::-1]


def reduce_yxz(shard_bits, replica_bits):
    return shard_bits[-1:] + replica_bits[::-1] + shard_bits[:-1][::-1]


def reduce_zxy(shard_bits, replica_bits):
    return shard_bits[-2:][::-1] + replica_bits + shard_bits[:-2][::-1]


def layout(lengths_row, token_rows):
    seq_ends = jnp.cumsum(lengths_row)
    positions = jnp.arange(token_rows, dtype=jnp.int32)
    passed = positions[:, None] >= seq_ends[None, :]
    segment = jnp.sum(passed.astype(jnp.int32), axis=1)
    seq_start = jnp.sum(jnp.where(passed, lengths_row[None, :], 0), axis=1)
    offset = (positions - seq_start).astype(jnp.float32)
    living = positions < seq_ends[-1]
    allowed = (
        (segment[:, None] == segment[None, :])
        & (positions[None, :] <= positions[:, None])
        & living[:, None]
    )
    allowed = allowed | (positions[:, None] == positions[None, :])
    return (offset, living.astype(jnp.float32), allowed)


def rotation(offset, half_dim):
    frequency = 10000.0 ** (-jnp.arange(half_dim, dtype=jnp.float32) / half_dim)
    angles = offset[:, None] * frequency[None, :]
    return (jnp.cos(angles)[:, None, :], jnp.sin(angles)[:, None, :])


def apply_rotary(values, cosine_table, sine_table):
    half_dim = values.shape[-1] // 2
    leading = values[..., :half_dim]
    trailing = values[..., half_dim:]
    return jnp.concatenate(
        [
            leading * cosine_table - trailing * sine_table,
            trailing * cosine_table + leading * sine_table,
        ],
        axis=-1,
    )


def reverse_rotary(gradient, cosine_table, sine_table):
    half_dim = gradient.shape[-1] // 2
    leading = gradient[..., :half_dim]
    trailing = gradient[..., half_dim:]
    return jnp.concatenate(
        [
            leading * cosine_table + trailing * sine_table,
            trailing * cosine_table - leading * sine_table,
        ],
        axis=-1,
    )


def rms_scale(values):
    return lax.rsqrt(jnp.mean(values * values, axis=-1, keepdims=True) + 1e-05)


def matrix_product(left, right):
    return jnp.dot(left, right, preferred_element_type=jnp.float32)


def rows_outer(left, right):
    return jnp.einsum("ra,rb->ab", left, right, preferred_element_type=jnp.float32)


def multiply_by_transpose(left, right):
    return jnp.einsum("rb,ab->ra", left, right, preferred_element_type=jnp.float32)


def norm_back(grad_unit, unit, scale):
    return scale * (grad_unit - unit * jnp.mean(grad_unit * unit, axis=-1, keepdims=True))


def body(
    tokens,
    cotangent,
    seq_lengths,
    w_query,
    key_weight,
    value_weight,
    w_out,
    w_gate,
    w_up,
    w_down,
    gain_attn,
    gain_ffn,
):
    token_rows = tokens.shape[0]
    shard_group = QUERY_HEADS // KEY_VALUE_HEADS
    offset, living, allowed = layout(seq_lengths[0], token_rows)
    cosine_table, sine_table = rotation(offset, HEAD_SIZE // 2)
    live_col = living[:, None]
    first = gather_rows(
        jnp.concatenate(
            [w_query, key_weight, value_weight, gain_attn[:, None], gain_ffn[:, None]], axis=1
        )
    )
    q_cols, kv_cols = w_query.shape[1], key_weight.shape[1]
    full_query = first[:, :q_cols]
    complete_key = first[:, q_cols : q_cols + kv_cols]
    complete_value = first[:, q_cols + kv_cols : q_cols + 2 * kv_cols]
    full_gain_attn = first[:, q_cols + 2 * kv_cols]
    full_gain_ffn = first[:, q_cols + 2 * kv_cols + 1]
    full_out = gather_rows(w_out)
    full_gate = gather_split(w_gate, False, gather_zxy)
    full_up = gather_split(w_up, False, gather_zyx)
    full_down = gather_split(w_down, True, gather_xyz)
    masked = tokens.astype(jnp.float32) * live_col
    scale_one = rms_scale(masked)
    unit_one = masked * scale_one
    normalized_input = (unit_one * full_gain_attn.astype(jnp.float32)).astype(jnp.bfloat16)
    query_rows = matrix_product(normalized_input, full_query).reshape(
        token_rows, QUERY_HEADS, HEAD_SIZE
    )
    unrotated_keys = matrix_product(normalized_input, complete_key).reshape(
        token_rows, KEY_VALUE_HEADS, HEAD_SIZE
    )
    projected_values = matrix_product(normalized_input, complete_value).reshape(
        token_rows, KEY_VALUE_HEADS, HEAD_SIZE
    )
    rotated_query = (
        apply_rotary(query_rows, cosine_table, sine_table)
        .astype(jnp.bfloat16)
        .reshape(token_rows, KEY_VALUE_HEADS, shard_group, HEAD_SIZE)
    )
    k_rot = apply_rotary(unrotated_keys, cosine_table, sine_table).astype(jnp.bfloat16)
    v_low = projected_values.astype(jnp.bfloat16)
    scores = (
        jnp.einsum("ikgd,jkd->kgij", rotated_query, k_rot, preferred_element_type=jnp.float32)
        * 0.125
    )
    shifted = jnp.where(allowed, scores, -1e30)
    peak = jnp.max(shifted, axis=-1, keepdims=True)
    raised = jnp.exp(shifted - peak)
    row_total = jnp.sum(raised, axis=-1, keepdims=True)
    probs = raised / row_total
    log_total = peak + jnp.log(row_total)
    attended = jnp.einsum(
        "kgij,jkd->ikgd", probs.astype(jnp.bfloat16), v_low, preferred_element_type=jnp.float32
    )
    attn_low = attended.reshape(token_rows, QUERY_HEADS * HEAD_SIZE).astype(jnp.bfloat16)
    middle = masked + matrix_product(attn_low, full_out)
    scale_two = rms_scale(middle)
    unit_two = middle * scale_two
    normed_two = (unit_two * full_gain_ffn.astype(jnp.float32)).astype(jnp.bfloat16)
    gate = matrix_product(normed_two, full_gate)
    up_proj = matrix_product(normed_two, full_up)
    sigmoid_gate = jax.nn.sigmoid(gate)
    silu_gate = gate * sigmoid_gate
    hidden = (silu_gate * up_proj).astype(jnp.bfloat16)
    ffn_out = matrix_product(hidden, full_down)
    output = (live_col * (middle + ffn_out)).astype(jnp.bfloat16)
    grad_rows = cotangent.astype(jnp.float32) * live_col
    grad_ffn = grad_rows.astype(jnp.bfloat16)
    grad_down_w = rows_outer(hidden, grad_ffn)
    grad_hidden = multiply_by_transpose(grad_ffn, full_down)
    grad_gate_low = (
        grad_hidden * up_proj * sigmoid_gate * (1.0 + gate * (1.0 - sigmoid_gate))
    ).astype(jnp.bfloat16)
    grad_up_low = (grad_hidden * silu_gate).astype(jnp.bfloat16)
    grad_gate_w = rows_outer(normed_two, grad_gate_low)
    grad_up_w = rows_outer(normed_two, grad_up_low)
    grad_normed_two = multiply_by_transpose(grad_gate_low, full_gate) + multiply_by_transpose(
        grad_up_low, full_up
    )
    grad_gain_two = jnp.sum(grad_normed_two * unit_two, axis=0)
    grad_middle = grad_rows + norm_back(
        grad_normed_two * full_gain_ffn.astype(jnp.float32), unit_two, scale_two
    )
    attention_gradient_reduced = grad_middle.astype(jnp.bfloat16)
    grad_out_w = rows_outer(attn_low, attention_gradient_reduced)
    grad_attended = (
        multiply_by_transpose(attention_gradient_reduced, full_out)
        .astype(jnp.bfloat16)
        .reshape(token_rows, KEY_VALUE_HEADS, shard_group, HEAD_SIZE)
    )
    scores_again = (
        jnp.einsum("ikgd,jkd->kgij", rotated_query, k_rot, preferred_element_type=jnp.float32)
        * 0.125
    )
    probs_again = jnp.exp(jnp.where(allowed, scores_again, -1e30) - log_total)
    probs_low = probs_again.astype(jnp.bfloat16)
    grad_probs = jnp.einsum(
        "ikgd,jkd->kgij", grad_attended, v_low, preferred_element_type=jnp.float32
    )
    row_delta = jnp.sum(probs_again * grad_probs, axis=-1, keepdims=True)
    grad_scores = (probs_again * (grad_probs - row_delta)).astype(jnp.bfloat16)
    grad_q_rot = (
        jnp.einsum("kgij,jkd->ikgd", grad_scores, k_rot, preferred_element_type=jnp.float32) * 0.125
    ).reshape(token_rows, QUERY_HEADS, HEAD_SIZE)
    rotated_key_gradient = (
        jnp.einsum("kgij,ikgd->jkd", grad_scores, rotated_query, preferred_element_type=jnp.float32)
        * 0.125
    )
    value_gradients = jnp.einsum(
        "kgij,ikgd->jkd", probs_low, grad_attended, preferred_element_type=jnp.float32
    )
    grad_queries = (
        reverse_rotary(grad_q_rot, cosine_table, sine_table)
        .astype(jnp.bfloat16)
        .reshape(token_rows, QUERY_HEADS * HEAD_SIZE)
    )
    grad_keys = (
        reverse_rotary(rotated_key_gradient, cosine_table, sine_table)
        .astype(jnp.bfloat16)
        .reshape(token_rows, KEY_VALUE_HEADS * HEAD_SIZE)
    )
    value_gradients_reduced = value_gradients.astype(jnp.bfloat16).reshape(
        token_rows, KEY_VALUE_HEADS * HEAD_SIZE
    )
    grad_query_w = rows_outer(normalized_input, grad_queries)
    grad_key_w = rows_outer(normalized_input, grad_keys)
    grad_value_w = rows_outer(normalized_input, value_gradients_reduced)
    grad_normed = (
        multiply_by_transpose(grad_queries, full_query)
        + multiply_by_transpose(grad_keys, complete_key)
        + multiply_by_transpose(value_gradients_reduced, complete_value)
    )
    grad_gain_one = jnp.sum(grad_normed * unit_one, axis=0)
    grad_input = live_col * (
        grad_middle
        + norm_back(grad_normed * full_gain_attn.astype(jnp.float32), unit_one, scale_one)
    )
    grad_tokens = grad_input.astype(jnp.bfloat16)
    sum_down = reduce_split(grad_down_w, True, reduce_xyz)
    sum_gate = reduce_split(grad_gate_w, False, reduce_yxz)
    sum_up = reduce_split(grad_up_w, False, reduce_zxy)
    sum_out = reduce_rows(grad_out_w)
    last = reduce_rows(
        jnp.concatenate(
            [
                grad_query_w,
                grad_key_w,
                grad_value_w,
                grad_gain_one[:, None],
                grad_gain_two[:, None],
            ],
            axis=1,
        )
    )
    return (
        output,
        grad_tokens,
        last[:, :q_cols],
        last[:, q_cols : q_cols + kv_cols],
        last[:, q_cols + kv_cols : q_cols + 2 * kv_cols],
        sum_out,
        sum_gate,
        sum_up,
        sum_down,
        last[:, q_cols + 2 * kv_cols],
        last[:, q_cols + 2 * kv_cols + 1],
    )


def solution(mesh):
    return jax.shard_map(
        body,
        mesh=mesh,
        in_specs=(
            P(("replica", "shard"), None),
            P(("replica", "shard"), None),
            P(("replica", "shard"), None),
            P("shard", None),
            P("shard", None),
            P("shard", None),
            P("shard", None),
            P("shard", None),
            P("shard", None),
            P("shard", None),
            P("shard"),
            P("shard"),
        ),
        out_specs=(
            P(("replica", "shard"), None),
            P(("replica", "shard"), None),
            P("shard", None),
            P("shard", None),
            P("shard", None),
            P("shard", None),
            P("shard", None),
            P("shard", None),
            P("shard", None),
            P("shard"),
            P("shard"),
        ),
        check_vma=False,
    )
```

```python
import jax
import jax.numpy as jnp
from jax import lax
from jax.experimental import pallas as pl
from jax.experimental.pallas import tpu as pltpu
from jax.sharding import PartitionSpec as P

QUERY_HEADS = 15
KEY_VALUE_HEADS = 5
HEAD_SIZE = 64


AXES = ("replica", "shard")


def cells():
    replicas = lax.axis_size("replica")
    shards = lax.axis_size("shard")
    return replicas, shards, lax.axis_index("replica"), lax.axis_index("shard")


def swap(value, kind, bit):
    replicas, shards, _, _ = cells()
    pairs = []
    for r in range(replicas):
        for s in range(shards):
            to = (r ^ bit) * shards + s if kind == "r" else r * shards + (s ^ bit)
            pairs.append((r * shards + s, to))
    return lax.ppermute(value, AXES, pairs)


def my_bit(kind, bit):
    _, _, r, s = cells()
    return ((r if kind == "r" else s) // bit) % 2


def bits_of(size):
    found = []
    bit = 1
    while bit < size:
        found.append(bit)
        bit *= 2
    return found


def low(value):
    return lax.reduce_precision(value.astype(jnp.float32), 8, 7).astype(jnp.bfloat16)


def grow(value, part, axis):
    other = swap(value, *part)
    upper = my_bit(*part) == 1
    first = jnp.where(upper, other, value)
    second = jnp.where(upper, value, other)
    return jnp.concatenate([first, second], axis=axis)


def add_low(mine, other):
    return low(mine.astype(jnp.float32) + other.astype(jnp.float32))


def halve(value, part, axis):
    upper = my_bit(*part) == 1
    lower_half = lax.slice_in_dim(value, 0, 1, axis=axis)
    upper_half = lax.slice_in_dim(value, 1, 2, axis=axis)
    keep = jnp.where(upper, upper_half, lower_half)
    send = jnp.where(upper, lower_half, upper_half)
    return add_low(keep, swap(send, *part))


def both(value, part):
    return add_low(value, swap(value, *part))


def shard_parts():
    _, shards, _, _ = cells()
    return [("s", bit) for bit in reversed(bits_of(shards))]


def replica_parts():
    replicas, _, _, _ = cells()
    return [("r", bit) for bit in reversed(bits_of(replicas))]


def gather_split(block, split_rows, order):
    shard_bits = shard_parts()
    replica_bits = replica_parts()
    replicas, shards, r, _ = cells()
    rows, columns = block.shape
    parts = shard_bits + replica_bits
    if split_rows:
        piece = lax.dynamic_slice_in_dim(block, r * (rows // replicas), rows // replicas, axis=0)
    else:
        piece = lax.dynamic_slice_in_dim(
            block, r * (columns // replicas), columns // replicas, axis=1
        )
    value = piece.reshape((1,) * len(parts) + piece.shape)
    for part in order(shard_bits, replica_bits):
        value = grow(value, part, parts.index(part))
        value = yield value
    value = value.reshape((shards, replicas) + piece.shape)
    if not split_rows:
        value = jnp.concatenate([value[:, i] for i in range(replicas)], axis=-1)
    yield value.reshape(shards * rows, columns)


def gather_rows(block):
    parts = shard_parts()
    value = block.reshape((1,) * len(parts) + block.shape)
    for part in parts:
        value = grow(value, part, parts.index(part))
        value = yield value
    yield value.reshape((-1, block.shape[1]))


def reduce_rows(grad):
    parts = shard_parts()
    _, shards, _, _ = cells()
    rows, columns = grad.shape
    value = grad.reshape((2,) * len(parts) + (rows // shards, columns))
    for part in reversed(parts):
        value = halve(value, part, parts.index(part))
        value = yield value
    value = value.reshape(rows // shards, columns)
    for part in replica_parts():
        value = both(value, part)
        value = yield value
    yield value.astype(jnp.float32)


def reduce_columns(left, right, half_bit, full_bits):
    parts = shard_parts()
    _, shards, _, _ = cells()
    rows, columns = left.shape
    shape = (2,) * len(parts) + (rows // shards, columns)
    core = parts[-1]
    axis = len(parts) - 1
    pair = (halve(left.reshape(shape), core, axis), halve(right.reshape(shape), core, axis))
    pair = yield pair
    upper = my_bit(*half_bit) == 1
    keep = jnp.where(upper, pair[1], pair[0])
    send = jnp.where(upper, pair[0], pair[1])
    value = add_low(keep, swap(send, *half_bit))
    value = yield value
    for part in reversed(parts[:-1]):
        value = halve(value, part, parts.index(part))
        value = yield value
    value = value.reshape(rows // shards, columns)
    for part in full_bits:
        value = both(value, part)
        value = yield value
    value = grow(value, half_bit, 1)
    value = yield value
    yield value.astype(jnp.float32)


class Flow:
    def __init__(self):
        self.running = []

    def add(self, steps):
        entry = [steps, None, False]
        self.running.append(entry)
        return entry

    def step(self, compute, inputs):
        moving = [e for e in self.running if not e[2]]
        held, inputs = lax.optimization_barrier(([e[1] for e in moving], inputs))
        for e, value in zip(moving, held):
            self.advance(e, value)
        result = list(compute(*inputs))
        moving = [e for e in moving if not e[2]]
        held, result[-1] = lax.optimization_barrier(([e[1] for e in moving], result[-1]))
        for e, value in zip(moving, held):
            e[1] = value
        return result

    def advance(self, entry, value):
        try:
            entry[1] = next(entry[0]) if value is None else entry[0].send(value)
        except StopIteration:
            entry[2] = True

    def finish(self, entry):
        while not entry[2]:
            self.advance(entry, entry[1])
        return entry[1]


def gather_zxy(shard_bits, replica_bits):
    return shard_bits[:-1] + replica_bits + shard_bits[-1:]


def gather_zyx(shard_bits, replica_bits):
    return shard_bits[:-1] + replica_bits[::-1] + shard_bits[-1:]


def gather_xyz(shard_bits, replica_bits):
    return shard_bits[:1] + replica_bits + shard_bits[1:]


def layout(lengths_row, token_rows):
    seq_ends = jnp.cumsum(lengths_row)
    positions = jnp.arange(token_rows, dtype=jnp.int32)
    passed = positions[:, None] >= seq_ends[None, :]
    segment = jnp.sum(passed.astype(jnp.int32), axis=1)
    seq_start = jnp.sum(jnp.where(passed, lengths_row[None, :], 0), axis=1)
    offset = (positions - seq_start).astype(jnp.float32)
    living = positions < seq_ends[-1]
    allowed = (
        (segment[:, None] == segment[None, :])
        & (positions[None, :] <= positions[:, None])
        & living[:, None]
    )
    allowed = allowed | (positions[:, None] == positions[None, :])
    return (offset, living.astype(jnp.float32), allowed)


def rotation(offset, half_dim):
    frequency = 10000.0 ** (-jnp.arange(half_dim, dtype=jnp.float32) / half_dim)
    angles = offset[:, None] * frequency[None, :]
    return (jnp.cos(angles)[:, None, :], jnp.sin(angles)[:, None, :])


def apply_rotary(values, cosine_table, sine_table):
    half_dim = values.shape[-1] // 2
    leading = values[..., :half_dim]
    trailing = values[..., half_dim:]
    return jnp.concatenate(
        [
            leading * cosine_table - trailing * sine_table,
            trailing * cosine_table + leading * sine_table,
        ],
        axis=-1,
    )


def reverse_rotary(gradient, cosine_table, sine_table):
    half_dim = gradient.shape[-1] // 2
    leading = gradient[..., :half_dim]
    trailing = gradient[..., half_dim:]
    return jnp.concatenate(
        [
            leading * cosine_table + trailing * sine_table,
            trailing * cosine_table - leading * sine_table,
        ],
        axis=-1,
    )


def rms_scale(values):
    return lax.rsqrt(jnp.mean(values * values, axis=-1, keepdims=True) + 1e-05)


def matrix_product(left, right):
    return jnp.dot(left, right, preferred_element_type=jnp.float32)


def rows_outer(left, right):
    return jnp.einsum("ra,rb->ab", left, right, preferred_element_type=jnp.float32)


def multiply_by_transpose(left, right):
    return jnp.einsum("rb,ab->ra", left, right, preferred_element_type=jnp.float32)


def norm_back(grad_unit, unit, scale):
    return scale * (grad_unit - unit * jnp.mean(grad_unit * unit, axis=-1, keepdims=True))


def row_block(rows):
    return 256 if rows % 256 == 0 else rows


def contract_last(left, right):
    return lax.dot_general(
        left, right, (((1,), (1,)), ((), ())), preferred_element_type=jnp.float32
    )


def contract_first(left, right):
    return lax.dot_general(
        left, right, (((0,), (0,)), ((), ())), preferred_element_type=jnp.float32
    )


def attend_kernel(q_ref, k_ref, v_ref, bias_ref, out_ref, lse_ref):
    group, rows = q_ref.shape[1], q_ref.shape[2]
    step = row_block(rows)
    for start in range(0, rows, step):
        reach = start + step
        keys = k_ref[0, :reach, :]
        values = v_ref[0, :reach, :]
        for head in range(group):
            scores = contract_last(q_ref[0, head, start:reach, :], keys) * 0.125
            scores = scores + bias_ref[start:reach, :reach]
            peak = jnp.max(scores, axis=-1, keepdims=True)
            raised = jnp.exp(scores - peak)
            total = jnp.sum(raised, axis=-1, keepdims=True)
            probs = (raised * (1.0 / total)).astype(jnp.bfloat16)
            out_ref[0, head, start:reach, :] = jnp.dot(
                probs, values, preferred_element_type=jnp.float32
            ).astype(jnp.bfloat16)
            lse_ref[0, start:reach, head : head + 1] = peak + jnp.log(total)


def unrope(value, cosine, sine):
    half = value.shape[-1] // 2
    swapped = jnp.concatenate([value[:, half:], value[:, :half]], axis=-1)
    return value * cosine + swapped * sine


def attend_back_kernel(
    q_ref, k_ref, v_ref, bias_ref, lse_ref, ga_ref, cos_ref, sin_ref, gq_ref, gk_ref, gv_ref, sk, sv
):
    group, rows = q_ref.shape[1], q_ref.shape[2]
    step = row_block(rows)
    sk[...] = jnp.zeros_like(sk)
    sv[...] = jnp.zeros_like(sv)
    for start in range(0, rows, step):
        reach = start + step
        keys = k_ref[0, :reach, :]
        values = v_ref[0, :reach, :]
        for head in range(group):
            queries = q_ref[0, head, start:reach, :]
            grads = ga_ref[0, head, start:reach, :]
            scores = contract_last(queries, keys) * 0.125 + bias_ref[start:reach, :reach]
            probs = jnp.exp(scores - lse_ref[0, start:reach, head : head + 1])
            grad_probs = contract_last(grads, values)
            delta = jnp.sum(probs * grad_probs, axis=-1, keepdims=True)
            grad_scores = (probs * (grad_probs - delta)).astype(jnp.bfloat16)
            grad_query = jnp.dot(grad_scores, keys, preferred_element_type=jnp.float32) * 0.125
            gq_ref[0, head, start:reach, :] = unrope(
                grad_query, cos_ref[start:reach, :], sin_ref[start:reach, :]
            ).astype(jnp.bfloat16)
            sk[:reach, :] += contract_first(grad_scores, queries)
            sv[:reach, :] += contract_first(probs.astype(jnp.bfloat16), grads)
    gk_ref[0] = unrope(sk[...] * 0.125, cos_ref[...], sin_ref[...]).astype(jnp.bfloat16)
    gv_ref[0] = sv[...].astype(jnp.bfloat16)


def head_spec(group, rows, size, base=0):
    return pl.BlockSpec((1, group, rows, size), lambda i: (i + base, 0, 0, 0))


def key_spec(rows, size, base=0):
    return pl.BlockSpec((1, rows, size), lambda i: (i + base, 0, 0))


def whole_spec(rows, columns):
    return pl.BlockSpec((rows, columns), lambda i: (0, 0))


def attend(query, key, value, bias, base, heads):
    _, group, rows, size = query.shape
    return pl.pallas_call(
        attend_kernel,
        grid=(heads,),
        in_specs=[
            head_spec(group, rows, size, base),
            key_spec(rows, size, base),
            key_spec(rows, size, base),
            whole_spec(rows, rows),
        ],
        out_specs=[head_spec(group, rows, size), key_spec(rows, group)],
        out_shape=[
            jax.ShapeDtypeStruct((heads, group, rows, size), jnp.bfloat16),
            jax.ShapeDtypeStruct((heads, rows, group), jnp.float32),
        ],
        compiler_params=pltpu.CompilerParams(vmem_limit_bytes=32 * 1024 * 1024),
        cost_estimate=pl.CostEstimate(
            flops=4 * heads * group * rows * rows * 256, bytes_accessed=12000000, transcendentals=0
        ),
    )(query, key, value, bias)


def attend_back(query, key, value, bias, lse, grad, cosine, sine, base, heads):
    _, group, rows, size = query.shape
    return pl.pallas_call(
        attend_back_kernel,
        grid=(heads,),
        in_specs=[
            head_spec(group, rows, size, base),
            key_spec(rows, size, base),
            key_spec(rows, size, base),
            whole_spec(rows, rows),
            key_spec(rows, group, base),
            head_spec(group, rows, size, base),
            whole_spec(rows, size),
            whole_spec(rows, size),
        ],
        out_specs=[head_spec(group, rows, size), key_spec(rows, size), key_spec(rows, size)],
        out_shape=[
            jax.ShapeDtypeStruct((heads, group, rows, size), jnp.bfloat16),
            jax.ShapeDtypeStruct((heads, rows, size), jnp.bfloat16),
            jax.ShapeDtypeStruct((heads, rows, size), jnp.bfloat16),
        ],
        scratch_shapes=[
            pltpu.VMEM((rows, size), jnp.float32),
            pltpu.VMEM((rows, size), jnp.float32),
        ],
        compiler_params=pltpu.CompilerParams(vmem_limit_bytes=32 * 1024 * 1024),
        cost_estimate=pl.CostEstimate(
            flops=10 * heads * group * rows * rows * 256, bytes_accessed=16000000, transcendentals=0
        ),
    )(query, key, value, bias, lse, grad, cosine, sine)


def body(
    tokens,
    cotangent,
    seq_lengths,
    w_query,
    key_weight,
    value_weight,
    w_out,
    w_gate,
    w_up,
    w_down,
    gain_attn,
    gain_ffn,
):
    token_rows = tokens.shape[0]
    shard_group = QUERY_HEADS // KEY_VALUE_HEADS
    offset, living, allowed = layout(seq_lengths[0], token_rows)
    cosine_table, sine_table = rotation(offset, HEAD_SIZE // 2)
    live_col = living[:, None]
    opening = Flow()
    first = opening.finish(opening.add(gather_rows(
        jnp.concatenate(
            [w_query, key_weight, value_weight, gain_attn[:, None], gain_ffn[:, None]], axis=1
        )
    )))
    q_cols, kv_cols = w_query.shape[1], key_weight.shape[1]
    full_query = first[:, :q_cols]
    complete_key = first[:, q_cols : q_cols + kv_cols]
    complete_value = first[:, q_cols + kv_cols : q_cols + 2 * kv_cols]
    full_gain_attn = first[:, q_cols + 2 * kv_cols]
    full_gain_ffn = first[:, q_cols + 2 * kv_cols + 1]
    full_gain_attn, w_out, w_gate, w_up, w_down = lax.optimization_barrier(
        (full_gain_attn, w_out, w_gate, w_up, w_down)
    )
    weights = Flow()
    coming_out = weights.add(gather_rows(w_out))
    coming_gate = weights.add(gather_split(w_gate, False, gather_zxy))
    coming_up = weights.add(gather_split(w_up, False, gather_zyx))
    coming_down = weights.add(gather_split(w_down, True, gather_xyz))
    masked = tokens.astype(jnp.float32) * live_col
    scale_one = rms_scale(masked)
    unit_one = masked * scale_one
    normalized_input = (unit_one * full_gain_attn.astype(jnp.float32)).astype(jnp.bfloat16)

    def project(normalized_input, full_query, complete_key, complete_value):
        query_rows = matrix_product(normalized_input, full_query).reshape(
            token_rows, QUERY_HEADS, HEAD_SIZE
        )
        unrotated_keys = matrix_product(normalized_input, complete_key).reshape(
            token_rows, KEY_VALUE_HEADS, HEAD_SIZE
        )
        projected_values = matrix_product(normalized_input, complete_value).reshape(
            token_rows, KEY_VALUE_HEADS, HEAD_SIZE
        )
        rotated_query = (
            apply_rotary(query_rows, cosine_table, sine_table)
            .astype(jnp.bfloat16)
            .reshape(token_rows, KEY_VALUE_HEADS, shard_group, HEAD_SIZE)
        )
        k_rot = apply_rotary(unrotated_keys, cosine_table, sine_table).astype(jnp.bfloat16)
        v_low = projected_values.astype(jnp.bfloat16)
        return (
            rotated_query.transpose(1, 2, 0, 3),
            k_rot.transpose(1, 0, 2),
            v_low.transpose(1, 0, 2),
        )

    heads_query, heads_key, heads_value = weights.step(
        lambda value: project(value, full_query, complete_key, complete_value), (normalized_input,)
    )
    bias = jnp.where(allowed, 0.0, -1e30).astype(jnp.float32)
    attended, log_total = [], []
    for base, heads in ((0, 1), (1, 2), (3, KEY_VALUE_HEADS - 3)):
        part, part_log = weights.step(
            lambda value: attend(heads_query, heads_key, value, bias, base, heads), (heads_value,)
        )
        attended.append(part)
        log_total.append(part_log)
    attended = jnp.concatenate(attended, axis=0)
    log_total = jnp.concatenate(log_total, axis=0)
    attn_low = attended.transpose(2, 0, 1, 3).reshape(token_rows, QUERY_HEADS * HEAD_SIZE)
    full_out = weights.finish(coming_out)
    full_gate = weights.finish(coming_gate)
    full_up = weights.finish(coming_up)
    full_down = weights.finish(coming_down)
    middle = masked + matrix_product(attn_low, full_out)
    scale_two = rms_scale(middle)
    unit_two = middle * scale_two
    normed_two = (unit_two * full_gain_ffn.astype(jnp.float32)).astype(jnp.bfloat16)
    gate = matrix_product(normed_two, full_gate)
    up_proj = matrix_product(normed_two, full_up)
    sigmoid_gate = jax.nn.sigmoid(gate)
    silu_gate = gate * sigmoid_gate
    hidden = (silu_gate * up_proj).astype(jnp.bfloat16)
    ffn_out = matrix_product(hidden, full_down)
    output = (live_col * (middle + ffn_out)).astype(jnp.bfloat16)
    grad_rows = cotangent.astype(jnp.float32) * live_col
    grad_ffn = grad_rows.astype(jnp.bfloat16)
    grads = Flow()
    replica_bits = replica_parts()
    sum_down = grads.add(reduce_rows(low(rows_outer(hidden, grad_ffn))))
    grad_hidden = multiply_by_transpose(grad_ffn, full_down)
    grad_gate_low = (
        grad_hidden * up_proj * sigmoid_gate * (1.0 + gate * (1.0 - sigmoid_gate))
    ).astype(jnp.bfloat16)
    grad_up_low = (grad_hidden * silu_gate).astype(jnp.bfloat16)
    half = grad_gate_low.shape[1] // 2
    sum_gate = grads.add(
        reduce_columns(
            low(rows_outer(normed_two, grad_gate_low[:, :half])),
            low(rows_outer(normed_two, grad_gate_low[:, half:])),
            replica_bits[0],
            replica_bits[1:],
        )
    )
    sum_up = grads.add(
        reduce_columns(
            low(rows_outer(normed_two, grad_up_low[:, :half])),
            low(rows_outer(normed_two, grad_up_low[:, half:])),
            replica_bits[-1],
            replica_bits[:-1],
        )
    )
    (grad_normed_two,) = grads.step(
        lambda up_low: (
            multiply_by_transpose(grad_gate_low, full_gate)
            + multiply_by_transpose(up_low, full_up),
        ),
        (grad_up_low,),
    )
    grad_gain_two = jnp.sum(grad_normed_two * unit_two, axis=0)
    grad_middle = grad_rows + norm_back(
        grad_normed_two * full_gain_ffn.astype(jnp.float32), unit_two, scale_two
    )
    attention_gradient_reduced = grad_middle.astype(jnp.bfloat16)
    sum_out = grads.add(reduce_rows(low(rows_outer(attn_low, attention_gradient_reduced))))
    grad_attended = (
        multiply_by_transpose(attention_gradient_reduced, full_out)
        .astype(jnp.bfloat16)
        .reshape(token_rows, KEY_VALUE_HEADS, shard_group, HEAD_SIZE)
    )
    both_cosine = jnp.concatenate([cosine_table[:, 0], cosine_table[:, 0]], axis=-1)
    both_sine = jnp.concatenate([sine_table[:, 0], -sine_table[:, 0]], axis=-1)
    inputs = (
        heads_query,
        heads_key,
        heads_value,
        bias,
        log_total,
        grad_attended.transpose(1, 2, 0, 3),
        both_cosine,
    )
    pieces = []
    for base, heads in ((0, 2), (2, 1), (3, 1), (4, KEY_VALUE_HEADS - 4)):
        pieces.append(grads.step(lambda sine: attend_back(*inputs, sine, base, heads), (both_sine,)))
    heads_gq, heads_gk, heads_gv = [jnp.concatenate(p, axis=0) for p in zip(*pieces)]
    grad_queries = heads_gq.transpose(2, 0, 1, 3).reshape(token_rows, QUERY_HEADS * HEAD_SIZE)
    grad_keys = heads_gk.transpose(1, 0, 2).reshape(token_rows, KEY_VALUE_HEADS * HEAD_SIZE)
    value_gradients_reduced = heads_gv.transpose(1, 0, 2).reshape(
        token_rows, KEY_VALUE_HEADS * HEAD_SIZE
    )
    grad_query_w = rows_outer(normalized_input, grad_queries)
    grad_key_w = rows_outer(normalized_input, grad_keys)
    grad_value_w = rows_outer(normalized_input, value_gradients_reduced)
    grad_normed = (
        multiply_by_transpose(grad_queries, full_query)
        + multiply_by_transpose(grad_keys, complete_key)
        + multiply_by_transpose(value_gradients_reduced, complete_value)
    )
    grad_gain_one = jnp.sum(grad_normed * unit_one, axis=0)
    grad_input = live_col * (
        grad_middle
        + norm_back(grad_normed * full_gain_attn.astype(jnp.float32), unit_one, scale_one)
    )
    grad_tokens = grad_input.astype(jnp.bfloat16)
    last = grads.add(reduce_rows(low(
        jnp.concatenate(
            [
                grad_query_w,
                grad_key_w,
                grad_value_w,
                grad_gain_one[:, None],
                grad_gain_two[:, None],
            ],
            axis=1,
        )
    )))
    last, sum_out, sum_gate, sum_up, sum_down = [
        grads.finish(e) for e in (last, sum_out, sum_gate, sum_up, sum_down)
    ]
    return (
        output,
        grad_tokens,
        last[:, :q_cols],
        last[:, q_cols : q_cols + kv_cols],
        last[:, q_cols + kv_cols : q_cols + 2 * kv_cols],
        sum_out,
        sum_gate,
        sum_up,
        sum_down,
        last[:, q_cols + 2 * kv_cols],
        last[:, q_cols + 2 * kv_cols + 1],
    )


def solution(mesh):
    return jax.shard_map(
        body,
        mesh=mesh,
        in_specs=(
            P(("replica", "shard"), None),
            P(("replica", "shard"), None),
            P(("replica", "shard"), None),
            P("shard", None),
            P("shard", None),
            P("shard", None),
            P("shard", None),
            P("shard", None),
            P("shard", None),
            P("shard", None),
            P("shard"),
            P("shard"),
        ),
        out_specs=(
            P(("replica", "shard"), None),
            P(("replica", "shard"), None),
            P("shard", None),
            P("shard", None),
            P("shard", None),
            P("shard", None),
            P("shard", None),
            P("shard", None),
            P("shard", None),
            P("shard"),
            P("shard"),
        ),
        check_vma=False,
    )
```
